256 devices in a mesh: sub: 8 (over x_hi, y), sens: 2 (over core), cell: 16 (over x_lo, z).
Axes of the slice: x: 4 (x_hi: 2, x_lo: 2; x = x_hi * 2 + x_lo), y: 4, z: 8, core: 2. Of those that a mesh axis runs over, the one named last changes fastest.
Arguments:
- snapshots: bfloat16 [8, 4, 2, 64, 1024], P('sub', None, None, 'cell', 'sens'), may hold values from -6 to 6
- sensor_modes: bfloat16 [8, 1024, 256], P('sub', 'sens'), may hold values from -8 to 8
- aperture_curvature: bfloat16 [8, 1024], P('sub', 'sens'), may hold values from 0 to 29952
- depth_offset: bfloat16 [8, 1024], P('sub', 'sens'), may hold values from -60 to 60
- cell_modes: bfloat16 [8, 4, 64, 2, 128, 128], P('sub', None, None, None, 'cell'), may hold values from -6 to 6
- ref_wavenumber: float32 [8, 4], P('sub'), may hold values from 0.3 to 0.7
- range_start: float32 [8], P('sub'), may hold values from 1000 to 3000
- mode_counts: int32 [8, 4], P('sub'), may hold values from 32 to 64, as said below
Outputs:
- ambiguity: float32 [4, 128, 128], P(None, 'cell', ('sub', 'sens'))
The draws below stay inside these ranges and needn't reach their ends.
Inputs may be any that keep to these rules, and one draw needn't show every extreme that they name: `mode_counts`: mode counts lie between half the table and the whole table; one entry equals 64.
All inputs are finite; a program needn't handle non-finite values.
Results may differ from the reference program's by a relative error of at most 0.0009.
Values may be sent and summed in bfloat16 or wider, within the bound.
No kernel may reach another device: no remote copies, remote signals or barrier semaphores. Data moves between devices by JAX's collectives and lax.ppermute only.
A program may use at most 128 MiB of HBM per device.

```python
import math
import jax
import jax.numpy as jnp
from jax import lax

H = 1024
M = 64
F = 4
T_SIZE = 64
NZ = 128
RB_DEV = 8
SUB = 8
NR = 128


def draw_sensor_modes(key, part):
    key = jax.random.fold_in(key, 11)
    normal_key, gain_key, column_key = jax.random.split(key, 3)
    normal_part = jnp.clip(jax.random.normal(normal_key, (SUB, H, F * M), jnp.float32), -6.0, 6.0)
    rise_factor = 2.0
    sensor_gain = jnp.exp(jax.random.uniform(gain_key, (SUB, H, 1), jnp.float32, 0.0, math.log(10.0)))
    column_gain = jnp.exp(jax.random.uniform(column_key, (SUB, 1, F * M), jnp.float32, 0.0, math.log(10.0)))
    position = (jnp.arange(SUB * H, dtype=jnp.int32).astype(jnp.float32) / (SUB * H - 1)).reshape(SUB, H, 1)
    values = normal_part * sensor_gain * column_gain * (1.0 + rise_factor * position) / (10.0 * math.sqrt(M))
    return jnp.clip(values, -8.0, 8.0).astype(jnp.bfloat16)


def draw_mode_counts(key, part):
    key = jax.random.fold_in(key, 23)
    count_key, place_key = jax.random.split(key)
    drawn = jax.random.randint(count_key, (SUB * F,), M // 2, M + 1, dtype=jnp.int32)
    chosen = jax.random.randint(place_key, (), 0, SUB * F, dtype=jnp.int32)
    drawn = jnp.where(jnp.arange(SUB * F, dtype=jnp.int32) == chosen, M, drawn)
    return drawn.reshape(SUB, F)


def block_scale(stream_key, extent, shards, least, largest):
    factor_of = 1.0
    for dim, parts in shards:
        steps = jax.random.uniform(jax.random.fold_in(jax.random.fold_in(stream_key, 6), dim), (parts,), jnp.float32, least / len(shards), largest / len(shards))
        factor_of = factor_of * jnp.repeat(jnp.exp(steps), extent[dim] // parts).reshape((-1,) + (1,) * (len(extent) - 1 - dim))
    return factor_of


def normal_values(key, extent, deviation, reach, cuts=(), held_as=jnp.bfloat16):
    result = jax.random.normal(key, extent, jnp.float32) * deviation
    if len(cuts) > 0:
        result = block_scale(key, extent, cuts, -0.22, 0.18) * result
    return jnp.clip(result, min=-reach, max=reach).astype(held_as)


def setup_inputs(seed: int = 0) -> dict:
    streams_of = jax.random.split(jax.random.key(seed), 9)
    return {
        "snapshots": normal_values(streams_of[0], (SUB, F, 2, T_SIZE, H), 1.0, 6.0, ((0, 8), (3, 16), (4, 2))),
        "sensor_modes": draw_sensor_modes(jax.random.fold_in(streams_of[8], 71), 0),
        "aperture_curvature": jnp.clip(29952.0 * jax.random.uniform(streams_of[2], (SUB, H), jnp.float32) ** block_scale(streams_of[2], (SUB, H), ((0, 8), (1, 2)), -0.2, 0.2), 0.0, 29952.0).astype(jnp.bfloat16),
        "depth_offset": jnp.clip(jax.random.uniform(streams_of[3], (SUB, H), jnp.float32, -60.0, 60.0) * block_scale(streams_of[3], (SUB, H), ((0, 8), (1, 2)), -0.4, 0.0), -60.0, 60.0).astype(jnp.bfloat16),
        "cell_modes": normal_values(streams_of[4], (SUB, F, M, 2, NR, NZ), 1.0, 6.0, ((0, 8), (4, 16))),
        "ref_wavenumber": jnp.clip(0.3 + 0.39999998 * jax.random.uniform(streams_of[5], (SUB, F), jnp.float32) ** block_scale(streams_of[5], (SUB, F), ((0, 8),), -0.2, 0.2), 0.3, 0.7),
        "range_start": jnp.clip(1000.0 + 2000.0 * jax.random.uniform(streams_of[6], (SUB,), jnp.float32) ** block_scale(streams_of[6], (SUB,), ((0, 8),), -0.2, 0.2), 1000.0, 3000.0),
        "mode_counts": draw_mode_counts(jax.random.fold_in(streams_of[8], 71), 0),
    }


range_step = 20.0
depth_step = 2.0
tiny = 1e-6


def replica_block(sensor_rows, curvature, offsets, modal_block, wavenumber, ranges, depths):
    mode_total = modal_block.shape[0]
    summed = jnp.dot(sensor_rows, modal_block.reshape(mode_total, -1), preferred_element_type=jnp.float32)
    summed = summed.reshape((sensor_rows.shape[0],) + modal_block.shape[1:])
    phase_term = wavenumber * (curvature[:, None, None] - offsets[:, None, None] * depths[None, None, :]) / ranges[None, :, None]
    cosine = jnp.cos(phase_term)
    sine_part = jnp.sin(phase_term)
    real_part = (summed[:, 0] * cosine - summed[:, 1] * sine_part).astype(jnp.bfloat16)
    imag_part = (summed[:, 0] * sine_part + summed[:, 1] * cosine).astype(jnp.bfloat16)
    energy = jnp.sum(jnp.square(real_part.astype(jnp.float32)) + jnp.square(imag_part.astype(jnp.float32)), axis=0)
    stacked = jnp.concatenate([real_part, imag_part], axis=0).reshape(2 * sensor_rows.shape[0], -1)
    return stacked, energy


def beam_rows(signal, stacked):
    real_x = signal[0]
    imag_x = signal[1]
    upper_rows = jnp.concatenate([real_x, imag_x], axis=1)
    lower_rows = jnp.concatenate([imag_x, -real_x], axis=1)
    return jnp.dot(jnp.concatenate([upper_rows, lower_rows], axis=0), stacked, preferred_element_type=jnp.float32)


def reference(snapshots, sensor_modes, aperture_curvature, depth_offset, cell_modes, ref_wavenumber, range_start, mode_counts):
    depths = depth_step * jnp.arange(NZ, dtype=jnp.int32).astype(jnp.float32)
    mode_index = jnp.arange(M, dtype=jnp.int32)

    def one_block(block_index):
        first_row = (block_index * RB_DEV).astype(jnp.int32)
        row_index = (first_row + jnp.arange(RB_DEV, dtype=jnp.int32)).astype(jnp.float32)
        beams = jnp.zeros((F, 2 * T_SIZE, RB_DEV * NZ), jnp.float32)
        energy = jnp.zeros((F, RB_DEV, NZ), jnp.float32)
        for array_index in range(SUB):
            ranges = range_start[array_index].astype(jnp.float32) + range_step * row_index
            curvature = aperture_curvature[array_index].astype(jnp.float32)
            offsets = depth_offset[array_index].astype(jnp.float32)
            window = lax.dynamic_slice_in_dim(cell_modes[array_index], first_row, RB_DEV, 3)
            beam_terms = []
            energy_terms = []
            for bin_index in range(F):
                kept_modes = (mode_index < mode_counts[array_index, bin_index]).astype(jnp.bfloat16)
                modal_block = window[bin_index] * kept_modes[:, None, None, None]
                sensor_rows = sensor_modes[array_index, :, bin_index * M:(bin_index + 1) * M]
                stacked, part_energy = replica_block(sensor_rows, curvature, offsets, modal_block, ref_wavenumber[array_index, bin_index], ranges, depths)
                beam_terms.append(beam_rows(snapshots[array_index, bin_index], stacked))
                energy_terms.append(part_energy)
            beams = beams + jnp.stack(beam_terms)
            energy = energy + jnp.stack(energy_terms)
        beams = beams.reshape(F, 2, T_SIZE, RB_DEV, NZ)
        power = jnp.mean(jnp.square(beams[:, 0]) + jnp.square(beams[:, 1]), axis=1)
        return 10.0 * jnp.log10((power + tiny) / (energy + tiny))

    blocks = lax.map(one_block, jnp.arange(NR // RB_DEV, dtype=jnp.int32))
    return jnp.transpose(blocks, (1, 0, 2, 3)).reshape(F, NR, NZ)
```

```python
import functools

import jax
import jax.numpy as jnp
from jax import lax
from jax.experimental import pallas as pl
from jax.experimental.pallas import tpu as pltpu
from jax.sharding import PartitionSpec as P

range_step = 20.0
depth_step = 2.0
tiny = 1e-06
Z0 = 8
f32 = jnp.float32
bf16 = jnp.bfloat16

NT = (((1,), (1,)), ((), ()))


def replica_kernel(
    bin_index,
    slots,
    counts,
    wave,
    first_range,
    cm,
    sensors,
    curv,
    offs,
    *rest,
):
    out, energy, a32, sums, e0c, e0s, e1c, e1s, esum = rest[-9:]
    modes = cm.shape[3]
    rows = cm.shape[2]
    depth = cm.shape[4]
    blocks = depth // Z0
    phones = sensors.shape[1]
    tile_rows = rows * Z0
    half = blocks * tile_rows

    for part in range(2):
        for row in range(rows):
            turned = cm[0, part, row].astype(f32).T
            a32[part, :, row] = turned.reshape(blocks, Z0, modes)
    lane = lax.broadcasted_iota(jnp.int32, (phones, modes), 1)
    taps = sensors[0, :, bin_index * modes : (bin_index + 1) * modes]
    taps = jnp.where(lane < counts[0, bin_index], taps.astype(f32), 0.0).astype(bf16)
    cells = a32[...].reshape(2 * half, modes).astype(bf16)
    sums[...] = lax.dot_general(cells, taps, NT, preferred_element_type=f32)

    shape = (rows, phones)
    ranges = first_range[0] + range_step * lax.broadcasted_iota(
        jnp.int32, shape, 0
    ).astype(f32)
    k = wave[0, bin_index]
    a = k * curv[...].astype(f32) / ranges
    b = k * (depth_step * offs[...].astype(f32)) / ranges
    zero = lax.broadcasted_iota(jnp.int32, (rows, Z0, phones), 1).astype(f32)
    low = (b[:, None, :] * zero).reshape(tile_rows, phones)
    e0c[...] = jnp.cos(low)
    e0s[...] = -jnp.sin(low)
    pc, ps = jnp.cos(a), jnp.sin(a)
    qc, qs = jnp.cos(Z0 * b), -jnp.sin(Z0 * b)
    for block in range(blocks):
        e1c[block] = pc
        e1s[block] = ps
        pc, ps = pc * qc - ps * qs, pc * qs + ps * qc

    def one_block(block, carry):
        first = pl.multiple_of(block * tile_rows, tile_rows)
        to = pl.multiple_of(slots[block] * tile_rows, tile_rows)
        total = jnp.zeros((tile_rows, 128), f32)
        for tile in range(phones // 128):
            cols = slice(tile * 128, (tile + 1) * 128)
            wide = (rows, Z0, 128)
            hc = jnp.broadcast_to(e1c[block, :, cols][:, None, :], wide).reshape(tile_rows, 128)
            hs = jnp.broadcast_to(e1s[block, :, cols][:, None, :], wide).reshape(tile_rows, 128)
            lc, ls = e0c[:, cols], e0s[:, cols]
            c = hc * lc - hs * ls
            s = hs * lc + hc * ls
            m0 = sums[pl.ds(first, tile_rows), cols]
            m1 = sums[pl.ds(half + first, tile_rows), cols]
            re = (m0 * c - m1 * s).astype(bf16)
            im = (m0 * s + m1 * c).astype(bf16)
            out[0, pl.ds(to, tile_rows), tile * 128 : (tile + 1) * 128] = re
            out[0, pl.ds(to, tile_rows), phones + tile * 128 : phones + (tile + 1) * 128] = im
            re, im = re.astype(f32), im.astype(f32)
            total = total + re * re + im * im
        esum[pl.ds(to, tile_rows), :] = total
        return carry

    lax.fori_loop(0, blocks, one_block, 0)
    total = esum[...]
    high = total.astype(bf16)
    rest_of = (total - high.astype(f32)).astype(bf16)
    ones = jnp.ones((8, 128), bf16)
    energy[...] = lax.dot_general(
        ones, high, NT, preferred_element_type=f32
    ) + lax.dot_general(ones, rest_of, NT, preferred_element_type=f32)


def replicas(bin_index, slots, counts, wave, first_range, cm, sensors, curv, offs, before):
    bins, _, rows, modes, depth = cm.shape
    phones = sensors.shape[1]
    blocks = depth // Z0
    cells = rows * depth
    smem = pl.BlockSpec(memory_space=pltpu.SMEM)
    vmem = pl.BlockSpec(memory_space=pltpu.VMEM)
    in_specs = [
        smem,
        smem,
        smem,
        smem,
        pl.BlockSpec((1, 2, rows, modes, depth), lambda i: (bin_index, 0, 0, 0, 0)),
        vmem,
        vmem,
        vmem,
    ]
    args = [slots, counts, wave, first_range, cm, sensors, curv, offs]
    aliases = {}
    if before is not None:
        in_specs.append(pl.BlockSpec(memory_space=pl.ANY))
        args.append(before)
        aliases = {len(args) - 1: 0}
    return pl.pallas_call(
        functools.partial(replica_kernel, bin_index),
        grid=(1,),
        in_specs=in_specs,
        out_specs=[
            pl.BlockSpec((1, cells, 2 * phones), lambda i: (bin_index, 0, 0)),
            vmem,
        ],
        out_shape=[
            jax.ShapeDtypeStruct((bins, cells, 2 * phones), bf16),
            jax.ShapeDtypeStruct((8, cells), f32),
        ],
        scratch_shapes=[
            pltpu.VMEM((2, blocks, rows, Z0, modes), f32),
            pltpu.VMEM((2 * cells, phones), f32),
            pltpu.VMEM((rows * Z0, phones), f32),
            pltpu.VMEM((rows * Z0, phones), f32),
            pltpu.VMEM((blocks, rows, phones), f32),
            pltpu.VMEM((blocks, rows, phones), f32),
            pltpu.VMEM((cells, 128), f32),
        ],
        input_output_aliases=aliases,
        compiler_params=pltpu.CompilerParams(vmem_limit_bytes=24 * 2**20),
        cost_estimate=pl.CostEstimate(
            flops=4 * cells * phones * modes, bytes_accessed=8 * 2**20, transcendentals=0
        ),
        name="replicas",
    )(*args)


def beam_kernel(pieces, *refs):
    w = refs[0]
    xs = refs[1 : 1 + pieces]
    keep, send = refs[1 + pieces :]
    real = jnp.concatenate([x[0, 0] for x in xs], axis=0)
    imag = jnp.concatenate([x[0, 1] for x in xs], axis=0)
    upper = jnp.concatenate([real, imag], axis=1)
    lower = jnp.concatenate([imag, -real], axis=1)
    signal = jnp.concatenate([upper, lower], axis=0)
    half = w.shape[1] // 2
    kept = lax.dot_general(w[0, :half], signal, NT, preferred_element_type=f32)
    sent = lax.dot_general(w[0, half:], signal, NT, preferred_element_type=f32)
    keep[:, 0] = kept.reshape(keep.shape[0], keep.shape[2], keep.shape[3])
    send[:, 0] = sent.reshape(send.shape[0], send.shape[2], send.shape[3]).astype(bf16)


def beams(w, pieces):
    bins, cells, depth = w.shape
    piece = pieces[0].shape
    looks = 2 * piece[2] * len(pieces)
    owners = 8
    tile_rows = cells // (2 * owners)
    out = (owners, bins, tile_rows, looks)
    block = (owners, 1, tile_rows, looks)
    return pl.pallas_call(
        functools.partial(beam_kernel, len(pieces)),
        grid=(bins,),
        in_specs=[pl.BlockSpec((1, cells, depth), lambda i: (i, 0, 0))]
        + [pl.BlockSpec((1,) + piece[1:], lambda i: (i, 0, 0, 0))] * len(pieces),
        out_specs=[pl.BlockSpec(block, lambda i: (0, i, 0, 0))] * 2,
        out_shape=[jax.ShapeDtypeStruct(out, f32), jax.ShapeDtypeStruct(out, bf16)],
        compiler_params=pltpu.CompilerParams(vmem_limit_bytes=24 * 2**20),
        cost_estimate=pl.CostEstimate(
            flops=2 * bins * cells * depth * looks,
            bytes_accessed=2 * bins * cells * depth,
            transcendentals=0,
        ),
        name="beams",
    )(w, *pieces)


def split(value):
    high = lax.reduce_precision(value, 8, 7)
    return high.astype(bf16), (value - high).astype(bf16)


def local(
    snapshots,
    sensor_modes,
    aperture_curvature,
    depth_offset,
    cell_modes,
    ref_wavenumber,
    range_start,
    mode_counts,
):
    _, bins, modes, _, rows, depth = cell_modes.shape
    blocks = depth // Z0
    cell = lax.axis_index("cell")
    sens = lax.axis_index("sens")
    first_range = range_start + range_step * (cell * rows).astype(f32)
    block_index = jnp.arange(blocks, dtype=jnp.int32)
    slots = ((block_index + sens) % 2) * (blocks // 2) + block_index // 2
    cm = jnp.transpose(cell_modes[0], (0, 2, 3, 1, 4))

    over_x = [(i, (i + 8) % 16) for i in range(16)]
    even = [(i, i ^ 1) for i in range(16)]
    odd = [(i, (i // 8) * 8 + ((i % 8 + (1 if i % 2 else -1)) % 8)) for i in range(16)]

    def after(value, done):
        return lax.optimization_barrier((value, done))[0]

    own = snapshots[0]
    w, energies = None, []

    def one_bin(bin_index, slots, w):
        w, energy = replicas(
            bin_index,
            slots,
            mode_counts,
            ref_wavenumber,
            first_range,
            cm,
            sensor_modes,
            aperture_curvature,
            depth_offset,
            w,
        )
        energies.append(energy[0])
        return w

    cell_pairs = (over_x, even, odd, even, odd)
    held = lax.optimization_barrier(own * jnp.ones((), bf16))
    piece, pieces = own, []
    for turn, pairs in enumerate(cell_pairs):
        got = lax.ppermute(piece, "cell", pairs)
        if turn == 0:
            cm = lax.optimization_barrier(cm)
        else:
            w = one_bin(turn - 1, after(slots, piece), w)
        got, w, cm = lax.optimization_barrier((got, w, cm))
        if turn < 2:
            held = jnp.concatenate([held, got], axis=2)
            piece = held
        else:
            piece = got
        if turn > 0:
            pieces.append(piece)
    energy = jnp.stack(energies).reshape(bins, 2, blocks // 2, rows * Z0)
    energy = jnp.transpose(energy, (1, 2, 0, 3)).reshape(2, blocks // 2, -1, 128)
    energy = energy[0] + lax.ppermute(energy[1], "sens", [(0, 1), (1, 0)])

    keep, send = beams(w, pieces)
    got = lax.ppermute(send, "sens", [(0, 1), (1, 0)])
    total = (keep + got.astype(f32)).astype(bf16)
    owners, looks = total.shape[0], total.shape[3]
    total = total.reshape(owners, -1, looks)
    high, low = split(energy)
    lines = energy.shape[1]
    pad = jnp.zeros((owners, 16 - 2 * lines, looks), bf16)
    total = jnp.concatenate([total, high, low, pad], axis=1)
    parts = lax.all_to_all(total, "sub", 0, 0)
    whole = jnp.sum(parts.astype(f32), axis=0)
    cells = bins * rows * Z0
    beam = whole[:cells]
    energy = (whole[cells : cells + lines] + whole[cells + lines : cells + 2 * lines]).reshape(
        bins, rows, Z0
    )
    power = jnp.sum(jnp.square(beam), axis=1).reshape(bins, rows, Z0) / (looks // 2)
    return 10.0 * jnp.log10((power + tiny) / (energy + tiny))


def solution(mesh):
    return jax.shard_map(
        local,
        mesh=mesh,
        in_specs=(
            P("sub", None, None, "cell", "sens"),
            P("sub", "sens", None),
            P("sub", "sens"),
            P("sub", "sens"),
            P("sub", None, None, None, "cell", None),
            P("sub", None),
            P("sub"),
            P("sub", None),
        ),
        out_specs=P(None, "cell", ("sub", "sens")),
        check_vma=False,
    )
```

```python
import functools

import jax
import jax.numpy as jnp
from jax import lax
from jax.experimental import pallas as pl
from jax.experimental.pallas import tpu as pltpu
from jax.sharding import PartitionSpec as P

range_step = 20.0
depth_step = 2.0
tiny = 1e-06
Z0 = 8
f32 = jnp.float32
bf16 = jnp.bfloat16

NT = (((1,), (1,)), ((), ()))


def small_sincos(r):
    t = r * r
    s = r + r * t * (-1.6666654611e-1 + t * (8.3321608736e-3 - t * 1.9515295891e-4))
    c = t * t * (4.166664568298827e-2 + t * (-1.388731625493765e-3 + t * 2.443315711809948e-5))
    return s, 1.0 - 0.5 * t + c


def sincos(x):
    turn = jnp.floor(x * 0.6366197723675814 + 0.5)
    r = ((x - turn * 1.5703125) - turn * 4.837512969970703e-4) - turn * 7.54978995489188e-8
    q = turn.astype(jnp.int32)
    s, c = small_sincos(r)
    odd = (q & 1) == 1
    sine, cosine = jnp.where(odd, c, s), jnp.where(odd, s, c)
    sine = jnp.where((q & 2) == 2, -sine, sine)
    cosine = jnp.where(((q + 1) & 2) == 2, -cosine, cosine)
    return sine, cosine


def replica_kernel(
    bin_index,
    slots,
    counts,
    wave,
    first_range,
    cm,
    sensors,
    curv,
    offs,
    *rest,
):
    out, energy, a32, sums, now_c, now_s, old_c, old_s, twice, esum, placed = rest
    modes = cm.shape[3]
    rows = cm.shape[2]
    depth = cm.shape[4]
    blocks = depth // Z0
    phones = sensors.shape[1]
    tile_rows = rows * Z0
    half = blocks * tile_rows

    for part in range(2):
        for row in range(rows):
            turned = cm[bin_index, part, row].astype(f32).T
            a32[part, :, row] = turned.reshape(blocks, Z0, modes)
    lane = lax.broadcasted_iota(jnp.int32, (phones, modes), 1)
    taps = sensors[0, :, bin_index * modes : (bin_index + 1) * modes]
    taps = jnp.where(lane < counts[0, bin_index], taps.astype(f32), 0.0).astype(bf16)
    cells = a32[...].reshape(2 * half, modes).astype(bf16)
    sums[...] = lax.dot_general(cells, taps, NT, preferred_element_type=f32)

    shape = (rows, phones)
    ranges = first_range[0] + range_step * lax.broadcasted_iota(
        jnp.int32, shape, 0
    ).astype(f32)
    k = wave[0, bin_index]
    a = k * curv[...].astype(f32) / ranges
    b = k * (depth_step * offs[...].astype(f32)) / ranges
    zero = lax.broadcasted_iota(jnp.int32, (rows, Z0, phones), 1).astype(f32)
    wide = (rows, Z0, phones)

    def spread(value):
        return jnp.broadcast_to(value[:, None, :], wide).reshape(tile_rows, phones)

    low_s, low_c = small_sincos((b[:, None, :] * zero).reshape(tile_rows, phones))
    high_s, high_c = (spread(v) for v in sincos(a))
    step_s, step_c = small_sincos(Z0 * b)
    c, s = high_c * low_c + high_s * low_s, high_s * low_c - high_c * low_s
    now_c[...], now_s[...] = c, s
    twice[...] = spread(2.0 * step_c)
    step_s, step_c = spread(step_s), spread(step_c)
    old_c[...], old_s[...] = c * step_c - s * step_s, s * step_c + c * step_s

    def one_pair(pair, carry):
        here = pl.ds(pl.multiple_of(pair * 2 * Z0, 2 * Z0), 2 * Z0)
        tiles = phones // 128
        group = 4
        for lead in range(0, tiles, group):
            spans = [slice(i * 128, (i + 1) * 128) for i in range(lead, lead + group)]
            turns = [(now_c[here, at], now_s[here, at]) for at in spans]
            before = [(old_c[here, at], old_s[here, at]) for at in spans]
            steps = [twice[here, at] for at in spans]
            for block in range(blocks):
                first = pl.multiple_of(block * tile_rows + pair * 2 * Z0, 2 * Z0)
                to = pl.multiple_of(slots[block] * tile_rows + pair * 2 * Z0, 2 * Z0)
                power = jnp.zeros((2 * Z0, 128), f32) if lead == 0 else esum[pl.ds(first, 2 * Z0), :]
                for i, at in enumerate(spans):
                    c, s = turns[i]
                    m0 = sums[pl.ds(first, 2 * Z0), at]
                    m1 = sums[pl.ds(half + first, 2 * Z0), at]
                    re = (m0 * c - m1 * s).astype(bf16)
                    im = (m0 * s + m1 * c).astype(bf16)
                    out[pl.ds(to, 2 * Z0), at] = re
                    out[pl.ds(to, 2 * Z0), phones + at.start : phones + at.stop] = im
                    power = power + (m0 * m0 + m1 * m1)
                    turns[i] = (steps[i] * c - before[i][0], steps[i] * s - before[i][1])
                    before[i] = (c, s)
                esum[pl.ds(first, 2 * Z0), :] = power
        return carry

    lax.fori_loop(0, rows // 2, one_pair, 0, unroll=True)
    for block in range(blocks):
        to = pl.multiple_of(slots[block] * tile_rows, tile_rows)
        placed[pl.ds(to, tile_rows), :] = esum[block * tile_rows : (block + 1) * tile_rows, :]
    total = placed[...]
    high = total.astype(bf16)
    rest_of = (total - high.astype(f32)).astype(bf16)
    ones = jnp.ones((8, 128), bf16)
    energy[...] = lax.dot_general(
        ones, high, NT, preferred_element_type=f32
    ) + lax.dot_general(ones, rest_of, NT, preferred_element_type=f32)


def replicas(bin_index, slots, counts, wave, first_range, cm, sensors, curv, offs):
    bins, _, rows, modes, depth = cm.shape
    phones = sensors.shape[1]
    blocks = depth // Z0
    cells = rows * depth
    smem = pl.BlockSpec(memory_space=pltpu.SMEM)
    vmem = pl.BlockSpec(memory_space=pltpu.VMEM)
    return pl.pallas_call(
        functools.partial(replica_kernel, bin_index),
        in_specs=[smem] * 4 + [vmem] * 4,
        out_specs=[vmem] * 2,
        out_shape=[
            jax.ShapeDtypeStruct((cells, 2 * phones), bf16),
            jax.ShapeDtypeStruct((8, cells), f32),
        ],
        scratch_shapes=[
            pltpu.VMEM((2, blocks, rows, Z0, modes), f32),
            pltpu.VMEM((2 * cells, phones), f32),
            *[pltpu.VMEM((rows * Z0, phones), f32)] * 5,
            *[pltpu.VMEM((cells, 128), f32)] * 2,
        ],
        compiler_params=pltpu.CompilerParams(vmem_limit_bytes=24 * 2**20),
        cost_estimate=pl.CostEstimate(
            flops=4 * cells * phones * modes, bytes_accessed=8 * 2**20, transcendentals=0
        ),
        name="replicas",
    )(slots, counts, wave, first_range, cm, sensors, curv, offs)


def beam_kernel(bins, *refs):
    ws, xs = refs[:bins], refs[bins:-2]
    keep, send = refs[-2:]
    for b, w in enumerate(ws):
        real = jnp.concatenate([x[b, 0] for x in xs], axis=0)
        imag = jnp.concatenate([x[b, 1] for x in xs], axis=0)
        upper = jnp.concatenate([real, imag], axis=1)
        lower = jnp.concatenate([imag, -real], axis=1)
        signal = jnp.concatenate([upper, lower], axis=0)
        half = w.shape[0] // 2
        kept = lax.dot_general(w[:half], signal, NT, preferred_element_type=f32)
        sent = lax.dot_general(w[half:], signal, NT, preferred_element_type=f32)
        keep[:, b] = kept.reshape(keep.shape[0], keep.shape[2], keep.shape[3])
        send[:, b] = sent.reshape(send.shape[0], send.shape[2], send.shape[3]).astype(bf16)


def beams(ws, pieces):
    bins = len(ws)
    cells, depth = ws[0].shape
    looks = 2 * pieces[0].shape[2] * len(pieces)
    owners = 8
    out = (owners, bins, cells // (2 * owners), looks)
    vmem = pl.BlockSpec(memory_space=pltpu.VMEM)
    return pl.pallas_call(
        functools.partial(beam_kernel, bins),
        in_specs=[vmem] * (bins + len(pieces)),
        out_specs=[vmem] * 2,
        out_shape=[jax.ShapeDtypeStruct(out, f32), jax.ShapeDtypeStruct(out, bf16)],
        compiler_params=pltpu.CompilerParams(vmem_limit_bytes=24 * 2**20),
        cost_estimate=pl.CostEstimate(
            flops=2 * bins * cells * depth * looks,
            bytes_accessed=2 * bins * cells * depth,
            transcendentals=0,
        ),
        name="beams",
    )(*ws, *pieces)


def split(value):
    high = lax.reduce_precision(value, 8, 7)
    return high.astype(bf16), (value - high).astype(bf16)


def local(
    snapshots,
    sensor_modes,
    aperture_curvature,
    depth_offset,
    cell_modes,
    ref_wavenumber,
    range_start,
    mode_counts,
):
    _, bins, modes, _, rows, depth = cell_modes.shape
    blocks = depth // Z0
    cell = lax.axis_index("cell")
    sens = lax.axis_index("sens")
    first_range = range_start + range_step * (cell * rows).astype(f32)
    block_index = jnp.arange(blocks, dtype=jnp.int32)
    sub = lax.axis_index("sub")

    away = block_index ^ (2 * sub + sens)
    slots = 8 * (away % 2) + 2 * ((away // 2) % 4) + away // 8
    cm = jnp.transpose(cell_modes[0], (0, 2, 3, 1, 4))

    def after(value, done):
        return lax.optimization_barrier((value, done))[0]

    own = snapshots[0]
    ws, energies = [], []

    def one_bin(bin_index, slots):
        w, energy = replicas(
            bin_index,
            slots,
            mode_counts,
            ref_wavenumber,
            first_range,
            cm,
            sensor_modes,
            aperture_curvature,
            depth_offset,
        )
        ws.append(w)
        energies.append(energy[0])

    def from_cell(piece, flip):
        return lax.ppermute(piece, "cell", [(i, i ^ flip) for i in range(16)])

    held = lax.optimization_barrier(own * jnp.ones((), bf16))
    gots = [from_cell(own, flip) for flip in (4, 6, 2)]
    one_bin(0, slots)
    gots, ws[0] = lax.optimization_barrier((gots, ws[0]))
    piece = jnp.concatenate([held, *gots], axis=2)
    gots = [from_cell(piece, flip) for flip in (9, 8, 1)]
    for bin_index in range(1, bins):
        one_bin(bin_index, after(slots, piece))
    gots, ws = lax.optimization_barrier((gots, ws))
    pieces = [piece, *gots]
    energy = jnp.stack(energies).reshape(bins, 2, blocks // 2, rows * Z0)
    energy = jnp.transpose(energy, (1, 2, 0, 3)).reshape(2, blocks // 2, -1, 128)
    energy = energy[0] + lax.ppermute(energy[1], "sens", [(0, 1), (1, 0)])

    keep, send = beams(ws, pieces)
    swap = [(0, 1), (1, 0)]
    got = lax.ppermute(send, "sens", swap)
    beam = keep + got.astype(f32)
    owners, looks = beam.shape[0], beam.shape[3]
    beam = beam.reshape(owners, -1, looks)
    cells, lines = beam.shape[1], energy.shape[1]
    def sent(part):
        high, low = split(energy[part])
        return jnp.concatenate([beam[part].astype(bf16), high, low], axis=1)

    def summed(total, got):
        beam, energy = total
        got = got.astype(f32)
        return (
            beam + got[:, :cells],
            energy + got[:, cells : cells + lines] + got[:, cells + lines :],
        )

    total = beam[0:2], energy[0:2]
    gots = [
        lax.ppermute(sent(slice(2 * k, 2 * k + 2)), "sub", [(i, i ^ k) for i in range(8)])
        for k in (2, 3, 1)
    ]
    for got in gots:
        total = summed(total, got)
    beam, energy = total
    got = lax.ppermute(sent(slice(1, 2)), "sub", [(i, i ^ 4) for i in range(8)])
    beam, energy = summed((beam[0:1], energy[0:1]), got)
    energy = energy.reshape(bins, rows, Z0)
    power = jnp.sum(jnp.square(beam[0]), axis=1).reshape(bins, rows, Z0) / (looks // 2)
    return 10.0 * jnp.log10((power + tiny) / (energy + tiny))


def solution(mesh):
    return jax.shard_map(
        local,
        mesh=mesh,
        in_specs=(
            P("sub", None, None, "cell", "sens"),
            P("sub", "sens", None),
            P("sub", "sens"),
            P("sub", "sens"),
            P("sub", None, None, None, "cell", None),
            P("sub", None),
            P("sub"),
            P("sub", None),
        ),
        out_specs=P(None, "cell", ("sub", "sens")),
        check_vma=False,
    )
```

```python
import functools

import jax
import jax.numpy as jnp
from jax import lax
from jax.experimental import pallas as pl
from jax.experimental.pallas import tpu as pltpu
from jax.sharding import PartitionSpec as P

range_step = 20.0
depth_step = 2.0
tiny = 1e-06
Z0 = 8
f32 = jnp.float32
bf16 = jnp.bfloat16

NT = (((1,), (1,)), ((), ()))


def small_sincos(r):
    t = r * r
    s = r + r * t * (-1.6666654611e-1 + t * (8.3321608736e-3 - t * 1.9515295891e-4))
    c = t * t * (4.166664568298827e-2 + t * (-1.388731625493765e-3 + t * 2.443315711809948e-5))
    return s, 1.0 - 0.5 * t + c


def sincos(x):
    turn = jnp.floor(x * 0.6366197723675814 + 0.5)
    r = ((x - turn * 1.5703125) - turn * 4.837512969970703e-4) - turn * 7.54978995489188e-8
    q = turn.astype(jnp.int32)
    s, c = small_sincos(r)
    odd = (q & 1) == 1
    sine, cosine = jnp.where(odd, c, s), jnp.where(odd, s, c)
    sine = jnp.where((q & 2) == 2, -sine, sine)
    cosine = jnp.where(((q + 1) & 2) == 2, -cosine, cosine)
    return sine, cosine


def replica_kernel(
    bin_index,
    slots,
    counts,
    wave,
    first_range,
    cm,
    sensors,
    curv,
    offs,
    *rest,
):
    out, energy, a32, sums, now_c, now_s, old_c, old_s, twice, esum = rest
    modes = cm.shape[3]
    rows = cm.shape[2]
    depth = cm.shape[4]
    blocks = depth // Z0
    phones = sensors.shape[1]
    tile_rows = rows * Z0
    half = blocks * tile_rows

    for part in range(2):
        for row in range(rows):
            turned = cm[bin_index, part, row].astype(f32).T
            a32[part, :, row] = turned.reshape(blocks, Z0, modes)
    lane = lax.broadcasted_iota(jnp.int32, (phones, modes), 1)
    taps = sensors[0, :, bin_index * modes : (bin_index + 1) * modes]
    taps = jnp.where(lane < counts[0, bin_index], taps.astype(f32), 0.0).astype(bf16)
    cells = a32[...].reshape(2 * half, modes).astype(bf16)
    sums[...] = lax.dot_general(cells, taps, NT, preferred_element_type=f32)

    shape = (rows, phones)
    ranges = first_range[0] + range_step * lax.broadcasted_iota(
        jnp.int32, shape, 0
    ).astype(f32)
    k = wave[0, bin_index]
    a = k * curv[...].astype(f32) / ranges
    b = k * (depth_step * offs[...].astype(f32)) / ranges
    zero = lax.broadcasted_iota(jnp.int32, (rows, Z0, phones), 1).astype(f32)
    wide = (rows, Z0, phones)

    def spread(value):
        return jnp.broadcast_to(value[:, None, :], wide).reshape(tile_rows, phones)

    low_s, low_c = small_sincos((b[:, None, :] * zero).reshape(tile_rows, phones))
    high_s, high_c = (spread(v) for v in sincos(a))
    step_s, step_c = small_sincos(Z0 * b)
    c, s = high_c * low_c + high_s * low_s, high_s * low_c - high_c * low_s
    now_c[...], now_s[...] = c, s
    twice[...] = spread(2.0 * step_c)
    step_s, step_c = spread(step_s), spread(step_c)
    old_c[...], old_s[...] = c * step_c - s * step_s, s * step_c + c * step_s

    def one_pair(pair, carry):
        here = pl.ds(pl.multiple_of(pair * 2 * Z0, 2 * Z0), 2 * Z0)
        if True:
            spans = [slice(i, i + 128) for i in range(0, phones, 128)]
            turns = [(now_c[here, at], now_s[here, at]) for at in spans]
            before = [(old_c[here, at], old_s[here, at]) for at in spans]
            steps = [twice[here, at] for at in spans]
            for block in range(blocks):
                first = pl.multiple_of(block * tile_rows + pair * 2 * Z0, 2 * Z0)
                to = pl.multiple_of(slots[block] * tile_rows + pair * 2 * Z0, 2 * Z0)
                power = jnp.zeros((2 * Z0, 128), f32)
                for i, at in enumerate(spans):
                    c, s = turns[i]
                    m0 = sums[pl.ds(first, 2 * Z0), at]
                    m1 = sums[pl.ds(half + first, 2 * Z0), at]
                    re = (m0 * c - m1 * s).astype(bf16)
                    im = (m0 * s + m1 * c).astype(bf16)
                    out[pl.ds(to, 2 * Z0), at] = re
                    out[pl.ds(to, 2 * Z0), phones + at.start : phones + at.stop] = im
                    power = power + (m0 * m0 + m1 * m1)
                    turns[i] = (steps[i] * c - before[i][0], steps[i] * s - before[i][1])
                    before[i] = (c, s)
                esum[pl.ds(to, 2 * Z0), :] = power
        return carry

    lax.fori_loop(0, rows // 2, one_pair, 0, unroll=True)
    for i in range(0, half, 128):
        line = jnp.sum(esum[i : i + 128, :].T, axis=0, keepdims=True)
        energy[:, i : i + 128] = jnp.broadcast_to(line, (8, 128))


def replicas(bin_index, slots, counts, wave, first_range, cm, sensors, curv, offs):
    bins, _, rows, modes, depth = cm.shape
    phones = sensors.shape[1]
    blocks = depth // Z0
    cells = rows * depth
    smem = pl.BlockSpec(memory_space=pltpu.SMEM)
    vmem = pl.BlockSpec(memory_space=pltpu.VMEM)
    return pl.pallas_call(
        functools.partial(replica_kernel, bin_index),
        in_specs=[smem] * 4 + [vmem] * 4,
        out_specs=[vmem] * 2,
        out_shape=[
            jax.ShapeDtypeStruct((cells, 2 * phones), bf16),
            jax.ShapeDtypeStruct((8, cells), f32),
        ],
        scratch_shapes=[
            pltpu.VMEM((2, blocks, rows, Z0, modes), f32),
            pltpu.VMEM((2 * cells, phones), f32),
            *[pltpu.VMEM((rows * Z0, phones), f32)] * 5,
            pltpu.VMEM((cells, 128), f32),
        ],
        compiler_params=pltpu.CompilerParams(vmem_limit_bytes=24 * 2**20),
        cost_estimate=pl.CostEstimate(
            flops=4 * cells * phones * modes, bytes_accessed=8 * 2**20, transcendentals=0
        ),
        name="replicas",
    )(slots, counts, wave, first_range, cm, sensors, curv, offs)


def beam_kernel(bins, *refs):
    ws, xs = refs[:bins], refs[bins:-2]
    keep, send = refs[-2:]
    for b, w in enumerate(ws):
        real = jnp.concatenate([x[b, 0] for x in xs], axis=0)
        imag = jnp.concatenate([x[b, 1] for x in xs], axis=0)
        upper = jnp.concatenate([real, imag], axis=1)
        lower = jnp.concatenate([imag, -real], axis=1)
        signal = jnp.concatenate([upper, lower], axis=0)
        half = w.shape[0] // 2
        kept = lax.dot_general(w[:half], signal, NT, preferred_element_type=f32)
        sent = lax.dot_general(w[half:], signal, NT, preferred_element_type=f32)
        keep[:, b] = kept.reshape(keep.shape[0], keep.shape[2], keep.shape[3])
        send[:, b] = sent.reshape(send.shape[0], send.shape[2], send.shape[3])


def beams(ws, pieces):
    bins = len(ws)
    cells, depth = ws[0].shape
    looks = 2 * pieces[0].shape[2] * len(pieces)
    owners = 8
    out = (owners, bins, cells // (2 * owners), looks)
    vmem = pl.BlockSpec(memory_space=pltpu.VMEM)
    return pl.pallas_call(
        functools.partial(beam_kernel, bins),
        in_specs=[vmem] * (bins + len(pieces)),
        out_specs=[vmem] * 2,
        out_shape=[jax.ShapeDtypeStruct(out, f32)] * 2,
        compiler_params=pltpu.CompilerParams(vmem_limit_bytes=24 * 2**20),
        cost_estimate=pl.CostEstimate(
            flops=2 * bins * cells * depth * looks,
            bytes_accessed=2 * bins * cells * depth,
            transcendentals=0,
        ),
        name="beams",
    )(*ws, *pieces)


def split(value):
    high = lax.reduce_precision(value, 8, 7)
    return high.astype(bf16), (value - high).astype(bf16)


def local(
    snapshots,
    sensor_modes,
    aperture_curvature,
    depth_offset,
    cell_modes,
    ref_wavenumber,
    range_start,
    mode_counts,
):
    _, bins, modes, _, rows, depth = cell_modes.shape
    blocks = depth // Z0
    cell = lax.axis_index("cell")
    sens = lax.axis_index("sens")
    first_range = range_start + range_step * (cell * rows).astype(f32)
    block_index = jnp.arange(blocks, dtype=jnp.int32)
    sub = lax.axis_index("sub")

    away = block_index ^ (2 * sub + sens)
    slots = 8 * (away % 2) + 2 * ((away // 2) % 4) + away // 8
    cm = jnp.transpose(cell_modes[0], (0, 2, 3, 1, 4))

    def after(value, done):
        return lax.optimization_barrier((value, done))[0]

    own = snapshots[0]
    ws, energies = [], []

    def one_bin(bin_index, slots):
        w, energy = replicas(
            bin_index,
            slots,
            mode_counts,
            ref_wavenumber,
            first_range,
            cm,
            sensor_modes,
            aperture_curvature,
            depth_offset,
        )
        ws.append(w)
        energies.append(energy[0])

    def from_cell(piece, flip):
        return lax.ppermute(piece, "cell", [(i, i ^ flip) for i in range(16)])

    held = lax.optimization_barrier(own * jnp.ones((), bf16))
    gots = [from_cell(own, flip) for flip in (4, 6, 2)]
    one_bin(0, slots)
    gots, ws[0] = lax.optimization_barrier((gots, ws[0]))
    piece = jnp.concatenate([held, *gots], axis=2)
    gots = [from_cell(piece, flip) for flip in (9, 8, 1)]
    for bin_index in range(1, bins):
        one_bin(bin_index, after(slots, piece))
    gots, ws = lax.optimization_barrier((gots, ws))
    pieces = [piece, *gots]
    energy = jnp.stack(energies).reshape(bins, 2, blocks // 2, rows * Z0)
    energy = jnp.transpose(energy, (1, 2, 0, 3)).reshape(2, blocks // 2, -1, 128)
    energy = energy[0] + lax.ppermute(energy[1], "sens", [(0, 1), (1, 0)])

    keep, send = beams(ws, pieces)
    swap = [(0, 1), (1, 0)]
    got = lax.ppermute(send, "sens", swap)
    beam = keep + got
    owners, looks = beam.shape[0], beam.shape[3]
    beam = beam.reshape(owners, -1, looks)
    cells, lines = beam.shape[1], energy.shape[1]
    def sent(part):
        high, low = split(energy[part])
        return jnp.concatenate([beam[part].astype(bf16), high, low], axis=1)

    def summed(total, got):
        beam, energy = total
        got = got.astype(f32)
        return (
            beam + got[:, :cells],
            energy + got[:, cells : cells + lines] + got[:, cells + lines :],
        )

    total = beam[0:2], energy[0:2]
    gots = [
        lax.ppermute(sent(slice(2 * k, 2 * k + 2)), "sub", [(i, i ^ k) for i in range(8)])
        for k in (2, 3, 1)
    ]
    for got in gots:
        total = summed(total, got)
    beam, energy = total
    got = lax.ppermute(sent(slice(1, 2)), "sub", [(i, i ^ 4) for i in range(8)])
    beam, energy = summed((beam[0:1], energy[0:1]), got)
    energy = energy.reshape(bins, rows, Z0)
    power = jnp.sum(jnp.square(beam[0]), axis=1).reshape(bins, rows, Z0) / (looks // 2)
    return 10.0 * jnp.log10((power + tiny) / (energy + tiny))


def solution(mesh):
    return jax.shard_map(
        local,
        mesh=mesh,
        in_specs=(
            P("sub", None, None, "cell", "sens"),
            P("sub", "sens", None),
            P("sub", "sens"),
            P("sub", "sens"),
            P("sub", None, None, None, "cell", None),
            P("sub", None),
            P("sub"),
            P("sub", None),
        ),
        out_specs=P(None, "cell", ("sub", "sens")),
        check_vma=False,
    )
```
